32 devices in a mesh: parts: 2 (over x), row: 16 (over z, y, core).
Axes of the slice: x: 2, y: 2, z: 4, core: 2. Of those that a mesh axis runs over, the one named last changes fastest.
Arguments:
- density: bfloat16 [39936, 936], P(('parts', 'row')), parts along dimension 0, may hold values from -0.59765625 to 0.59765625
- tile_mask: int32 [384, 9], P('parts'), parts along dimension 0, may hold values from 0 to 1, as said below
- padding: int32 [384], P('parts'), parts along dimension 0, may hold values from 0 to 26
Outputs:
- purified: bfloat16 [39936, 936], P(('parts', 'row')), parts along dimension 0
The draws below stay inside these ranges and needn't reach their ends.
There are 2 independent parts, one for each index of `parts`. The reference program is written for one: setup_inputs(seed, part) draws one part's arguments, and reference() takes and returns one part's arrays. A program takes and returns all parts, laid end to end along the dimension named above; each array names one. Nothing has to cross between parts.
Inputs may be any that keep to these rules, and one draw needn't show every extreme that they name: `tile_mask`: centre column 4 is 1 in every row; entries whose tile column i + c - 4 falls outside 0 to 191 are 0.
All inputs are finite; a program needn't handle non-finite values.
Results may differ from the reference program's by a relative error of at most 0.006.
Values may be sent and summed in bfloat16 or wider, within the bound.
A program may use at most 128 MiB of HBM per device.

```python
import jax
import jax.numpy as jnp
from jax import lax

B = 104
H = 4
BAND = 9
NT = 192
ORD = 19968


def draw_tile_mask(key, part):
    key = jax.random.fold_in(key, 7)
    tiles = jnp.arange(NT, dtype=jnp.int32)[:, None]
    offsets = jnp.arange(BAND, dtype=jnp.int32)[None, :]
    region = tiles // max(NT // 6, 1) % 3
    threshold = 35 + 25 * region
    rolls = jax.random.randint(key, (NT, BAND), 0, 100, dtype=jnp.int32)
    chosen = jnp.where(offsets == H, 1, (rolls < threshold).astype(jnp.int32))
    column = tiles + offsets - H
    inside = (column >= 0) & (column < NT)
    return jnp.where(inside, chosen, 0).astype(jnp.int32)


def with_ends(entries, own_key, least, top_value):
    index_at = [jax.random.randint(jax.random.fold_in(own_key, axis), (), 0, length) for axis, length in enumerate(entries.shape)]
    longest = entries.shape.index(max(entries.shape))
    next_to = index_at[:longest] + [(index_at[longest] + 1) % entries.shape[longest]] + index_at[longest + 1:]
    return entries.at[tuple(index_at)].set(least).at[tuple(next_to)].set(top_value)


def levels(own_key, shape, shards, smallest, largest):
    factor_of, own = 1.0, jax.random.fold_in(own_key, 6)
    for axis_at, blocks in shards:
        steps = jnp.exp(jax.random.uniform(jax.random.fold_in(own, axis_at), (blocks,), jnp.float32, smallest / len(shards), largest / len(shards)))
        factor_of = factor_of * jnp.repeat(steps, shape[axis_at] // blocks).reshape([-1 if axis == axis_at else 1 for axis in range(len(shape))])
    return factor_of


def gaussian(own_key, dims, scale, reach, cuts=(), kind=jnp.bfloat16):
    result = scale * jax.random.normal(own_key, dims, jnp.float32)
    if cuts:
        result = result * levels(own_key, dims, cuts, -0.22, 0.18)
    return jnp.clip(result, -reach, reach).astype(kind)


def setup_inputs(seed: int = 0, part: int = 0) -> dict:
    arg_keys = jax.random.split(jax.random.key(seed), 4)
    part_keys = jax.random.split(jax.random.fold_in(arg_keys[3], part), 4)
    density = gaussian(part_keys[0], (ORD, BAND * B), 0.1, 0.59765625, ((0, 16),))
    tile_mask = draw_tile_mask(jax.random.fold_in(jax.random.fold_in(arg_keys[3], part), 71), part)
    padding = with_ends(jax.random.randint(part_keys[2], (NT,), 0, B // 4 + 1), jax.random.fold_in(part_keys[2], 1), 0, (B // 4 + 1) - 1).astype(jnp.int32)
    return {"density": density, "tile_mask": tile_mask, "padding": padding}


def tile_row(left_row, window):
    widened = jnp.pad(window, ((0, 0), (0, 0), (H, H), (0, 0)))
    stacked = jnp.stack([widened[a, :, 2 * H - a:2 * H - a + BAND, :] for a in range(BAND)], axis=0)
    return jnp.einsum("xay,aycz->xcz", left_row.astype(jnp.float32), stacked.astype(jnp.float32))


def band_product(left_rows, source):
    padded = jnp.pad(source, ((H, H), (0, 0), (0, 0), (0, 0)))

    def one_row(index):
        window = lax.dynamic_slice_in_dim(padded, index, BAND, 0)
        row_tile = lax.dynamic_index_in_dim(left_rows, index, 0, keepdims=False)
        return tile_row(row_tile, window)

    return lax.map(one_row, jnp.arange(left_rows.shape[0], dtype=jnp.int32))


def reference(density, tile_mask, padding):
    slots = jnp.arange(B, dtype=jnp.int32)
    usable = (slots[None, :] < (B - padding)[:, None]).astype(jnp.bfloat16)
    usable_padded = jnp.pad(usable, ((H, H), (0, 0)))
    col_usable = jnp.stack([usable_padded[c:c + NT] for c in range(BAND)], axis=1)
    kept_tiles = tile_mask.astype(jnp.bfloat16)[:, None, :, None]
    dense = density.reshape(NT, B, BAND, B)
    filtered = dense * kept_tiles * usable[:, :, None, None] * col_usable[:, None, :, :]
    square = (band_product(filtered, filtered) * kept_tiles.astype(jnp.float32)).astype(jnp.bfloat16)
    cubed = band_product(filtered, square) * kept_tiles.astype(jnp.float32)
    purified = 3.0 * square.astype(jnp.float32) - 2.0 * cubed
    return purified.astype(jnp.bfloat16).reshape(NT * B, BAND * B)
```

```python
import functools

import jax
import jax.numpy as jnp
from jax import lax
from jax.experimental import pallas as pl
from jax.experimental.pallas import tpu as pltpu
from jax.sharding import PartitionSpec as P

B = 104
H = 4
BAND = 9
PR = 2 * B
PW = 256
NP = 5
WIDE = NP * PW
FAR = 4
OWN = 6
ALL = OWN + 2 * FAR
MESH = pl.DeviceIdType.MESH


def kernel(count, tiles, density, tile_mask, padding, out, x, f, s, t32, cm,
           send_sem, recv_sem, own_sem):
    me = lax.axis_index("row")
    odd = lax.rem(me, 2)
    even = odd == 0
    has_up = me > 0
    has_down = me < count - 1
    first = me * (2 * OWN) - 2 * FAR

    own = pltpu.make_async_copy(density, x.at[pl.ds(FAR * PR, OWN * PR), :], own_sem)
    own.start()

    barrier = pltpu.get_barrier_semaphore()

    @pl.when(has_up)
    def _():
        pl.semaphore_signal(barrier, inc=1, device_id={"row": me - 1}, device_id_type=MESH)

    @pl.when(has_down)
    def _():
        pl.semaphore_signal(barrier, inc=1, device_id={"row": me + 1}, device_id_type=MESH)

    pl.semaphore_wait(barrier, has_up.astype(jnp.int32) + has_down.astype(jnp.int32))

    def piece(src_row, dst_row, rows, lane, width, slot, where):
        return pltpu.make_async_remote_copy(
            src_ref=density.at[pl.ds(src_row, rows), pl.ds(lane, width)],
            dst_ref=x.at[pl.ds(dst_row, rows), pl.ds(lane, width)],
            send_sem=send_sem.at[slot], recv_sem=recv_sem.at[slot],
            device_id={"row": where}, device_id_type=MESH)

    full = BAND * B

    def tail():
        return [piece(4 * PR, 2 * PR, 2 * PR, 0, full, 0, me + 1),
                piece(3 * PR, 1 * PR, PR, 512, full - 512, 1, me + 1),
                piece(2 * PR, 0, PR, 640, full - 640, 2, me + 1)]

    def head():
        return [piece(0, 10 * PR, 2 * PR, 0, full, 3, me - 1),
                piece(2 * PR, 12 * PR, PR, 0, 512, 4, me - 1),
                piece(3 * PR, 13 * PR, PR, 0, 256, 5, me - 1)]

    @pl.when(has_down)
    def _():
        for c in tail():
            c.start()

    @pl.when(has_up)
    def _():
        for c in head():
            c.start()

    lane = lax.broadcasted_iota(jnp.int32, (1, WIDE), 1)
    inner = lane % PW
    second = (inner >= B).astype(jnp.int32)
    slot_of = (lane // PW) * 2 + second
    z = inner - B * second

    def masks(p, carry):
        for a in range(2):
            t = first + 2 * p + a
            tc = jnp.clip(t, 0, tiles - 1)
            lim = jnp.zeros((1, WIDE), jnp.int32)
            for c in range(BAND):
                j = jnp.clip(t + c - H, 0, tiles - 1)
                lim = jnp.where(slot_of == a + c, tile_mask[tc, c] * (B - padding[j]), lim)
            cm[pl.ds(pl.multiple_of(p * 16 + a * 8, 8), 8), :] = jnp.broadcast_to(
                jnp.where((z < lim) & (z < B), 1.0, 0.0), (8, WIDE))
        return carry

    lax.fori_loop(0, ALL, masks, 0)
    t32[...] = jnp.zeros_like(t32)
    f[...] = jnp.zeros_like(f)

    def mask_row(p, a):
        return cm[pl.ds(pl.multiple_of(p * 16 + a * 8, 8), 1), :]

    def rows_of(p):
        return pl.ds(pl.multiple_of(p * PR, 16), PR)

    row = lax.broadcasted_iota(jnp.int32, (B, 1), 0)

    def load(p):
        band = x[rows_of(p), :].astype(jnp.float32)
        for m in range(NP):
            w = min(PR, BAND * B - m * PR)
            t32[0:B, m * PW:m * PW + w] = band[0:B, m * PR:m * PR + w]
        t32[B:PR, B:PR] = band[B:PR, 0:B]
        for m in range(1, NP):
            t32[B:PR, m * PW:m * PW + PR] = band[B:PR, m * PR - B:m * PR + B]
        half = []
        for a in range(2):
            t = jnp.clip(first + 2 * p + a, 0, tiles - 1)
            ok = jnp.where(row < B - padding[t], 1.0, 0.0)
            m = ok * mask_row(p, a)
            half.append(jnp.where(m > 0.5, t32[a * B:(a + 1) * B, :], 0.0))
        f[rows_of(p), :] = jnp.concatenate(half, axis=0).astype(jnp.bfloat16)

    def product(p, right, jj):
        total = None
        for kk in range(max(0, jj - 2), min(NP, jj + 3)):
            c = jj - kk + 2
            term = jnp.dot(f[rows_of(p), kk * PW:kk * PW + PR],
                           right[rows_of(p - 2 + kk), c * PW:(c + 1) * PW],
                           preferred_element_type=jnp.float32)
            total = term if total is None else total + term
        return total

    def both(p, jj):
        cols = slice(jj * PW, (jj + 1) * PW)
        return jnp.concatenate(
            [jnp.broadcast_to(mask_row(p, a)[:, cols], (B, PW)) for a in range(2)], axis=0)

    def square(p):
        for jj in range(NP):
            s[rows_of(p), jj * PW:(jj + 1) * PW] = (
                product(p, f, jj) * both(p, jj)).astype(jnp.bfloat16)

    def cubed(p):
        for jj in range(NP):
            cols = slice(jj * PW, (jj + 1) * PW)
            c = product(p, s, jj) * both(p, jj)
            t32[:, cols] = 3.0 * s[rows_of(p), cols].astype(jnp.float32) - 2.0 * c
        top = [t32[0:B, m * PW:m * PW + min(PR, BAND * B - m * PR)] for m in range(NP)]
        low = [t32[B:PR, B:PR]] + [t32[B:PR, m * PW:m * PW + PR] for m in range(1, NP)]
        whole = jnp.concatenate(
            [jnp.concatenate(top, axis=1), jnp.concatenate(low, axis=1)], axis=0)
        out[pl.ds(pl.multiple_of((p - FAR) * PR, 16), PR), :] = whole.astype(jnp.bfloat16)

    def at(p):
        return p + odd * (ALL - 1 - 2 * p)

    def run(body, pairs):
        lo, hi = pairs
        step = 1 if hi >= lo else -1

        def go(i, carry):
            body(at(lo + step * i))
            return carry

        lax.fori_loop(0, abs(hi - lo) + 1, go, 0)

    own.wait()
    run(load, (4, 9))
    run(square, (6, 7))

    def wait_below():
        for c in head():
            c.wait_recv()

    def wait_above():
        for c in tail():
            c.wait_recv()

    pl.when(even)(wait_below)
    pl.when(jnp.logical_not(even))(wait_above)
    run(load, (10, 13))
    run(square, (8, 11))
    run(cubed, (8, 9))

    @pl.when(even & has_up)
    def _():
        wait_above()

    @pl.when(jnp.logical_not(even) & has_down)
    def _():
        wait_below()

    @pl.when((even & has_up) | (jnp.logical_not(even) & has_down))
    def _():
        run(load, (3, 0))

    run(square, (5, 2))
    run(cubed, (7, 4))

    @pl.when(has_down)
    def _():
        for c in tail():
            c.wait_send()

    @pl.when(has_up)
    def _():
        for c in head():
            c.wait_send()


def per_device(density, tile_mask, padding):
    count = lax.axis_size("row")
    rows = density.shape[0]
    assert rows == OWN * PR
    body = functools.partial(kernel, count, tile_mask.shape[0])
    return pl.pallas_call(
        body,
        out_shape=jax.ShapeDtypeStruct(density.shape, jnp.bfloat16),
        in_specs=[
            pl.BlockSpec(memory_space=pl.ANY),
            pl.BlockSpec(memory_space=pltpu.SMEM),
            pl.BlockSpec(memory_space=pltpu.SMEM),
        ],
        out_specs=pl.BlockSpec(memory_space=pltpu.VMEM),
        scratch_shapes=[
            pltpu.VMEM((ALL * PR, BAND * B), jnp.bfloat16),
            pltpu.VMEM((ALL * PR, WIDE), jnp.bfloat16),
            pltpu.VMEM((ALL * PR, WIDE), jnp.bfloat16),
            pltpu.VMEM((PR, WIDE), jnp.float32),
            pltpu.VMEM((ALL * 16, WIDE), jnp.float32),
            pltpu.SemaphoreType.DMA((6,)),
            pltpu.SemaphoreType.DMA((6,)),
            pltpu.SemaphoreType.DMA,
        ],
        compiler_params=pltpu.CompilerParams(
            collective_id=0, has_side_effects=True, vmem_limit_bytes=52 * 1024 * 1024),
    )(density, tile_mask, padding)


def solution(mesh):
    return jax.shard_map(
        per_device,
        mesh=mesh,
        in_specs=(P(("parts", "row"), None), P("parts", None), P("parts")),
        out_specs=P(("parts", "row"), None),
        check_vma=False,
    )
```

```python
import functools

import jax
import jax.numpy as jnp
from jax import lax
from jax.experimental import pallas as pl
from jax.experimental.pallas import tpu as pltpu
from jax.sharding import PartitionSpec as P

B = 104
H = 4
BAND = 9
PR = 2 * B
PW = 256
NP = 5
TALL = NP * PR
FULL = BAND * B
FAR = 4
OWN = 6
ALL = OWN + 2 * FAR
SKIP = (OWN * PR - FAR * PR) // 128 * 128
SIDE = 896
LAST = OWN * PR - SKIP
MESH = pl.DeviceIdType.MESH


def kernel(count, tiles, density, tile_mask, padding, out, x, up, down, f, s, t32, lv,
           send_sem, recv_sem, own_sem):
    me = lax.axis_index("row")
    odd = lax.rem(me, 2)
    even = odd == 0
    has_up = me > 0
    has_down = me < count - 1
    first = me * (2 * OWN) - 2 * FAR

    own = pltpu.make_async_copy(density, x, own_sem)
    own.start()

    barrier = pltpu.get_barrier_semaphore()

    @pl.when(has_up)
    def _():
        pl.semaphore_signal(barrier, inc=1, device_id={"row": me - 1}, device_id_type=MESH)

    @pl.when(has_down)
    def _():
        pl.semaphore_signal(barrier, inc=1, device_id={"row": me + 1}, device_id_type=MESH)

    pl.semaphore_wait(barrier, has_up.astype(jnp.int32) + has_down.astype(jnp.int32))

    def piece(row, rows, lane, width, dst, back, slot, where):
        return pltpu.make_async_remote_copy(
            src_ref=density.at[pl.ds(row, rows), pl.ds(lane, width)],
            dst_ref=dst.at[pl.ds(row, rows), pl.ds(lane - back, width)],
            send_sem=send_sem.at[slot], recv_sem=recv_sem.at[slot],
            device_id={"row": where}, device_id_type=MESH)

    def tail():
        return [piece(0, FULL, 768, 480, up, SKIP, 0, me + 1),
                piece(512, FULL - 512, 640, 128, up, SKIP, 1, me + 1),
                piece(624, FULL - 624, 512, 128, up, SKIP, 2, me + 1),
                piece(832, FULL - 832, 384, 128, up, SKIP, 3, me + 1)]

    def head():
        return [piece(0, FULL, 0, 512, down, 0, 4, me - 1),
                piece(0, 416, 512, 128, down, 0, 5, me - 1),
                piece(0, 208, 640, 128, down, 0, 6, me - 1),
                piece(0, 112, 768, 128, down, 0, 7, me - 1)]

    @pl.when(has_down)
    def _():
        for c in tail():
            c.start()

    @pl.when(has_up)
    def _():
        for c in head():
            c.start()

    lane = lax.broadcasted_iota(jnp.int32, (1, PW), 1)
    second = lane >= B

    def limits(p, carry):
        t = first + 2 * p
        tc = [jnp.clip(t + a, 0, tiles - 1) for a in range(2)]
        ok = ((lane < B - padding[tc[0]]) & (lane < B)) | (
            second & (lane < PR - padding[tc[1]]))
        for slot in range(2 * NP):
            room = B - padding[jnp.clip(t + slot - H, 0, tiles - 1)]
            top = tile_mask[slot, tc[0]] * room if slot < BAND else 0
            low = tile_mask[slot - 1, tc[1]] * room if slot else 0
            row = jnp.where(ok, jnp.where(second, low, top), 0)
            lv[pl.ds(pl.multiple_of((p * 2 * NP + slot) * 8, 8), 8), :] = (
                jnp.broadcast_to(row, (8, PW)))
        return carry

    lax.fori_loop(0, ALL, limits, 0)
    t32[...] = jnp.zeros_like(t32)
    f[...] = jnp.zeros_like(f)
    z = lax.broadcasted_iota(jnp.int32, (B, PW), 0)

    def masked(p, slot, block):
        row = lv[pl.ds(pl.multiple_of((p * 2 * NP + slot) * 8, 8), 1), :]
        return jnp.where(z < row, block, 0.0)

    def load(p):
        for q in range(ALL):
            if q < FAR:
                src, lo = up, OWN * PR - FAR * PR - SKIP + q * PR
            elif q < FAR + OWN:
                src, lo = x, (q - FAR) * PR
            else:
                src, lo = down, (q - FAR - OWN) * PR

            @pl.when(p == q)
            def _(src=src, lo=lo):
                t32[0:FULL, 0:PR] = src[:, lo:lo + PR].astype(jnp.float32)

        for m in range(NP):
            half = []
            for slot in (2 * m, 2 * m + 1):
                at_top = min(slot, BAND - 1) * B
                at_low = max(slot - 1, 0) * B
                both = jnp.where(second, t32[at_low:at_low + B, :], t32[at_top:at_top + B, :])
                half.append(masked(p, slot, both))
            f[p, m * PR:(m + 1) * PR, :] = jnp.concatenate(half, axis=0).astype(jnp.bfloat16)

    def product(p, left, jj):
        total = None
        for kk in range(max(0, jj - 2), min(NP, jj + 3)):
            c = jj - kk + 2
            term = jnp.dot(left[p - 2 + kk, c * PR:(c + 1) * PR, 0:PR],
                           f[p, kk * PR:(kk + 1) * PR, :],
                           preferred_element_type=jnp.float32)
            total = term if total is None else total + term
        return jnp.concatenate(
            [masked(p, 2 * jj + a, total[a * B:(a + 1) * B, :]) for a in range(2)], axis=0)

    def square(p):
        for jj in range(NP):
            s[p, jj * PR:(jj + 1) * PR, :] = product(p, f, jj).astype(jnp.bfloat16)

    def cubed(p):
        for jj in range(NP):
            rows = slice(jj * PR, (jj + 1) * PR)
            t32[rows, :] = 3.0 * s[p, rows, :].astype(jnp.float32) - 2.0 * product(p, s, jj)
        whole = jnp.where(second, t32[B:TALL, :], t32[0:FULL, :]).astype(jnp.bfloat16)
        for q in range(OWN):
            @pl.when(p == q + FAR)
            def _(q=q):
                out[:, q * PR:(q + 1) * PR] = whole[:, 0:PR]

    def at(p):
        return p + odd * (ALL - 1 - 2 * p)

    def run(body, pairs):
        lo, hi = pairs
        step = 1 if hi >= lo else -1

        def go(i, carry):
            body(at(lo + step * i))
            return carry

        lax.fori_loop(0, abs(hi - lo) + 1, go, 0)

    own.wait()
    run(load, (4, 9))
    run(square, (6, 7))

    def wait_below():
        for c in head():
            c.wait_recv()

    def wait_above():
        for c in tail():
            c.wait_recv()

    pl.when(even)(wait_below)
    pl.when(jnp.logical_not(even))(wait_above)
    run(load, (10, 13))
    run(square, (8, 11))
    run(cubed, (8, 9))

    @pl.when(even & has_up)
    def _():
        wait_above()

    @pl.when(jnp.logical_not(even) & has_down)
    def _():
        wait_below()

    @pl.when((even & has_up) | (jnp.logical_not(even) & has_down))
    def _():
        run(load, (3, 0))

    run(square, (5, 2))
    run(cubed, (7, 4))

    @pl.when(has_down)
    def _():
        for c in tail():
            c.wait_send()

    @pl.when(has_up)
    def _():
        for c in head():
            c.wait_send()


def per_device(density, tile_mask, padding):
    count = lax.axis_size("row")
    rows = density.shape[0]
    assert rows == OWN * PR
    body = functools.partial(kernel, count, tile_mask.shape[0])
    return pl.pallas_call(
        body,
        out_shape=jax.ShapeDtypeStruct((FULL, rows), jnp.bfloat16),
        in_specs=[
            pl.BlockSpec(memory_space=pl.ANY),
            pl.BlockSpec(memory_space=pltpu.SMEM),
            pl.BlockSpec(memory_space=pltpu.SMEM),
        ],
        out_specs=pl.BlockSpec(memory_space=pltpu.VMEM),
        scratch_shapes=[
            pltpu.VMEM((FULL, OWN * PR), jnp.bfloat16),
            pltpu.VMEM((FULL, LAST), jnp.bfloat16),
            pltpu.VMEM((FULL, SIDE), jnp.bfloat16),
            pltpu.VMEM((ALL, TALL, PW), jnp.bfloat16),
            pltpu.VMEM((ALL, TALL, PW), jnp.bfloat16),
            pltpu.VMEM((TALL, PW), jnp.float32),
            pltpu.VMEM((ALL * 2 * NP * 8, PW), jnp.int32),
            pltpu.SemaphoreType.DMA((8,)),
            pltpu.SemaphoreType.DMA((8,)),
            pltpu.SemaphoreType.DMA,
        ],
        compiler_params=pltpu.CompilerParams(
            collective_id=0, has_side_effects=True, vmem_limit_bytes=52 * 1024 * 1024),
    )(density.T, tile_mask.T, padding).T


def solution(mesh):
    return jax.shard_map(
        per_device,
        mesh=mesh,
        in_specs=(P(("parts", "row"), None), P("parts", None), P("parts")),
        out_specs=P(("parts", "row"), None),
        check_vma=False,
    )
```

```python
import functools

import jax
import jax.numpy as jnp
from jax import lax
from jax.experimental import pallas as pl
from jax.experimental.pallas import tpu as pltpu
from jax.sharding import PartitionSpec as P

B = 104
H = 4
BAND = 9
PR = 2 * B
PW = 256
NP = 5
TALL = NP * PR
FULL = BAND * B
FAR = 4
OWN = 6
ALL = OWN + 2 * FAR
SKIP = (OWN * PR - FAR * PR) // 128 * 128
SIDE = 896
LAST = OWN * PR - SKIP
MESH = pl.DeviceIdType.MESH


def kernel(count, tiles, density, tile_mask, padding, out, x, up, down, f, s, t32, lv,
           send_sem, recv_sem, own_sem):
    me = lax.axis_index("row")
    odd = lax.rem(me, 2)
    even = odd == 0
    has_up = me > 0
    has_down = me < count - 1
    first = me * (2 * OWN) - 2 * FAR

    own = pltpu.make_async_copy(density, x, own_sem)
    own.start()

    barrier = pltpu.get_barrier_semaphore()

    @pl.when(has_up)
    def _():
        pl.semaphore_signal(barrier, inc=1, device_id={"row": me - 1}, device_id_type=MESH)

    @pl.when(has_down)
    def _():
        pl.semaphore_signal(barrier, inc=1, device_id={"row": me + 1}, device_id_type=MESH)

    pl.semaphore_wait(barrier, has_up.astype(jnp.int32) + has_down.astype(jnp.int32))

    def piece(row, rows, lane, width, dst, back, slot, where):
        return pltpu.make_async_remote_copy(
            src_ref=density.at[pl.ds(row, rows), pl.ds(lane, width)],
            dst_ref=dst.at[pl.ds(row, rows), pl.ds(lane - back, width)],
            send_sem=send_sem.at[slot], recv_sem=recv_sem.at[slot],
            device_id={"row": where}, device_id_type=MESH)

    def tail():
        return [[piece(0, FULL, 1024, 224, up, SKIP, 0, me + 1)],
                [piece(0, FULL, 768, 256, up, SKIP, 1, me + 1)],
                [piece(512, FULL - 512, 640, 128, up, SKIP, 2, me + 1),
                 piece(624, FULL - 624, 512, 128, up, SKIP, 3, me + 1)],
                [piece(832, FULL - 832, 384, 128, up, SKIP, 4, me + 1)]]

    def head():
        return [[piece(0, FULL, 0, 256, down, 0, 5, me - 1)],
                [piece(0, FULL, 256, 256, down, 0, 6, me - 1)],
                [piece(0, 416, 512, 128, down, 0, 7, me - 1),
                 piece(0, 208, 640, 128, down, 0, 8, me - 1)],
                [piece(0, 112, 768, 128, down, 0, 9, me - 1)]]

    def each(stages):
        return [c for stage in stages for c in stage]

    @pl.when(has_down)
    def _():
        for c in each(tail()):
            c.start()

    @pl.when(has_up)
    def _():
        for c in each(head()):
            c.start()

    lane = lax.broadcasted_iota(jnp.int32, (1, PW), 1)
    second = lane >= B

    def limits(p, carry):
        t = first + 2 * p
        tc = [jnp.clip(t + a, 0, tiles - 1) for a in range(2)]
        ok = ((lane < B - padding[tc[0]]) & (lane < B)) | (
            second & (lane < PR - padding[tc[1]]))
        for slot in range(2 * NP):
            room = B - padding[jnp.clip(t + slot - H, 0, tiles - 1)]
            top = tile_mask[slot, tc[0]] * room if slot < BAND else 0
            low = tile_mask[slot - 1, tc[1]] * room if slot else 0
            row = jnp.where(ok, jnp.where(second, low, top), 0)
            lv[pl.ds(pl.multiple_of((p * 2 * NP + slot) * 8, 8), 8), :] = (
                jnp.broadcast_to(row, (8, PW)))
        return carry

    lax.fori_loop(0, ALL, limits, 0)
    t32[...] = jnp.zeros_like(t32)
    f[...] = jnp.zeros_like(f)
    z = lax.broadcasted_iota(jnp.int32, (B, PW), 0)

    def masked(p, slot, block):
        row = lv[pl.ds(pl.multiple_of((p * 2 * NP + slot) * 8, 8), 1), :]
        return jnp.where(z < row, block, 0.0)

    def load(p):
        for q in range(ALL):
            if q < FAR:
                src, lo = up, OWN * PR - FAR * PR - SKIP + q * PR
            elif q < FAR + OWN:
                src, lo = x, (q - FAR) * PR
            else:
                src, lo = down, (q - FAR - OWN) * PR

            @pl.when(p == q)
            def _(src=src, lo=lo):
                t32[0:FULL, 0:PR] = src[:, lo:lo + PR].astype(jnp.float32)

        for m in range(NP):
            half = []
            for slot in (2 * m, 2 * m + 1):
                at_top = min(slot, BAND - 1) * B
                at_low = max(slot - 1, 0) * B
                both = jnp.where(second, t32[at_low:at_low + B, :], t32[at_top:at_top + B, :])
                half.append(masked(p, slot, both))
            f[p, m * PR:(m + 1) * PR, :] = jnp.concatenate(half, axis=0).astype(jnp.bfloat16)

    def product(p, left, jj):
        total = None
        for kk in range(max(0, jj - 2), min(NP, jj + 3)):
            c = jj - kk + 2
            term = jnp.dot(left[p - 2 + kk, c * PR:(c + 1) * PR, 0:PR],
                           f[p, kk * PR:(kk + 1) * PR, :],
                           preferred_element_type=jnp.float32)
            total = term if total is None else total + term
        return jnp.concatenate(
            [masked(p, 2 * jj + a, total[a * B:(a + 1) * B, :]) for a in range(2)], axis=0)

    def square(p):
        for jj in range(NP):
            s[p, jj * PR:(jj + 1) * PR, :] = product(p, f, jj).astype(jnp.bfloat16)

    def cubed(p):
        for jj in range(NP):
            rows = slice(jj * PR, (jj + 1) * PR)
            t32[rows, :] = 3.0 * s[p, rows, :].astype(jnp.float32) - 2.0 * product(p, s, jj)
        whole = jnp.where(second, t32[B:TALL, :], t32[0:FULL, :]).astype(jnp.bfloat16)
        for q in range(OWN):
            @pl.when(p == q + FAR)
            def _(q=q):
                out[:, q * PR:(q + 1) * PR] = whole[:, 0:PR]

    def at(p):
        return p + odd * (ALL - 1 - 2 * p)

    def run(body, pairs):
        lo, hi = pairs
        step = 1 if hi >= lo else -1

        def go(i, carry):
            body(at(lo + step * i))
            return carry

        lax.fori_loop(0, abs(hi - lo) + 1, go, 0)

    own.wait()
    run(load, (4, 9))
    run(square, (6, 7))

    def wait_below():
        for c in each(head()):
            c.wait_recv()

    def wait_above():
        for c in each(tail()):
            c.wait_recv()

    pl.when(even)(wait_below)
    pl.when(jnp.logical_not(even))(wait_above)
    run(load, (10, 13))
    run(square, (8, 11))
    run(cubed, (8, 9))

    from_above = even & has_up
    from_below = jnp.logical_not(even) & has_down

    def stage(i, carry):
        for k in range(FAR):
            @pl.when(from_above & (i == k))
            def _(k=k):
                for c in tail()[k]:
                    c.wait_recv()

            @pl.when(from_below & (i == k))
            def _(k=k):
                for c in head()[k]:
                    c.wait_recv()

        @pl.when(from_above | from_below)
        def _():
            load(at(FAR - 1 - i))

        square(at(FAR + 1 - i))
        cubed(at(FAR + 3 - i))
        return carry

    lax.fori_loop(0, FAR, stage, 0)

    @pl.when(has_down)
    def _():
        for c in each(tail()):
            c.wait_send()

    @pl.when(has_up)
    def _():
        for c in each(head()):
            c.wait_send()


def per_device(density, tile_mask, padding):
    count = lax.axis_size("row")
    rows = density.shape[0]
    assert rows == OWN * PR
    body = functools.partial(kernel, count, tile_mask.shape[0])
    return pl.pallas_call(
        body,
        out_shape=jax.ShapeDtypeStruct((FULL, rows), jnp.bfloat16),
        in_specs=[
            pl.BlockSpec(memory_space=pl.ANY),
            pl.BlockSpec(memory_space=pltpu.SMEM),
            pl.BlockSpec(memory_space=pltpu.SMEM),
        ],
        out_specs=pl.BlockSpec(memory_space=pltpu.VMEM),
        scratch_shapes=[
            pltpu.VMEM((FULL, OWN * PR), jnp.bfloat16),
            pltpu.VMEM((FULL, LAST), jnp.bfloat16),
            pltpu.VMEM((FULL, SIDE), jnp.bfloat16),
            pltpu.VMEM((ALL, TALL, PW), jnp.bfloat16),
            pltpu.VMEM((ALL, TALL, PW), jnp.bfloat16),
            pltpu.VMEM((TALL, PW), jnp.float32),
            pltpu.VMEM((ALL * 2 * NP * 8, PW), jnp.int32),
            pltpu.SemaphoreType.DMA((10,)),
            pltpu.SemaphoreType.DMA((10,)),
            pltpu.SemaphoreType.DMA,
        ],
        compiler_params=pltpu.CompilerParams(
            collective_id=0, has_side_effects=True, vmem_limit_bytes=52 * 1024 * 1024),
    )(density.T, tile_mask.T, padding).T


def solution(mesh):
    return jax.shard_map(
        per_device,
        mesh=mesh,
        in_specs=(P(("parts", "row"), None), P("parts", None), P("parts")),
        out_specs=P(("parts", "row"), None),
        check_vma=False,
    )
```
